512 devices in a mesh: row: 64 (over y_hi, z, core), col: 8 (over y_lo, x).
Axes of the slice: x: 4, y: 4 (y_hi: 2, y_lo: 2; y = y_hi * 2 + y_lo), z: 16, core: 2. Of those that a mesh axis runs over, the one named last changes fastest.
Arguments:
- graph_tiles: bfloat16 [512, 8, 19, 128, 128], P('row', 'col'), may hold values from -0.0234375 to 0.0234375
- tile_cols: int32 [512, 8, 19], P('row', 'col'), may hold values from 0 to 511, as said below
- tile_counts: int32 [512, 8], P('row', 'col'), may hold values from 0 to 19, as said below
- pair_order: int32 [256], replicated, may hold values from 0 to 255, as said below
- sketch: bfloat16 [512, 128, 128], P(('row', 'col')), may hold values from -6 to 6
- degree_scale: float32 [512, 128], P(('row', 'col')), may hold values from 0.4 to 2.5
Outputs:
- sketch_basis: float32 [512, 128, 128], P(('row', 'col'))
- core_matrix: float32 [128, 128], replicated
The draws below stay inside these ranges and needn't reach their ends.
Inputs may be any that keep to these rules, and one draw needn't show every extreme that they name: `pair_order`: a permutation of the pair indices. `tile_counts`: at most 19, the most is reached. `tile_cols`: natural block numbers. For slots s < tile_counts[q, c]: distinct within (q, c), at most the natural block of held row q, and the column's held position h satisfies (h) % 8 = c. Other slots hold arbitrary block numbers and are ignored.
All inputs are finite; a program needn't handle non-finite values.
Results may differ from the reference program's by a relative error of at most 0.0022.
Values may be sent and summed in bfloat16 or wider, within the bound.
No kernel may reach another device: no remote copies, remote signals or barrier semaphores. Data moves between devices by JAX's collectives and lax.ppermute only.
A program may use at most 64 MiB of HBM per device.

```python
import math
import jax
import jax.numpy as jnp
from jax import lax

TILE = 128
RANK = 128
SLOTS = 19
COLS = 8
BLOCKS = 512
PAIRS = 256
SHARD_BLOCKS = 1
NODES = 65536
N_COL = 8


def fold_pattern(key):
    pair_order = jax.random.permutation(key, PAIRS).astype(jnp.int32)
    slot_of = jnp.zeros((PAIRS,), jnp.int32).at[pair_order].set(jnp.arange(PAIRS, dtype=jnp.int32))
    blocks = jnp.arange(BLOCKS, dtype=jnp.int32)
    lower_end = jnp.minimum(blocks, BLOCKS - 1 - blocks)
    held_pos = 2 * slot_of[lower_end] + (blocks >= PAIRS).astype(jnp.int32)
    column_of = held_pos // SHARD_BLOCKS % COLS
    natural = jnp.where(blocks % 2 == 0, pair_order[blocks // 2], BLOCKS - 1 - pair_order[blocks // 2])
    col_ids = jnp.arange(COLS, dtype=jnp.int32)
    eligible = (blocks[None, None, :] <= natural[:, None, None]) & (column_of[None, None, :] == col_ids[None, :, None])
    reach_count = jnp.sum(eligible.astype(jnp.int32), axis=-1)
    spread = jax.random.randint(jax.random.fold_in(key, 1), (BLOCKS, COLS), 2, 5).astype(jnp.int32)
    spread = jnp.where(natural[:, None] == BLOCKS - 1, 4, spread)
    counts = reach_count * SLOTS * spread // (4 * (BLOCKS // COLS))
    noise_bits = jax.random.randint(jax.random.fold_in(key, 2), (BLOCKS, COLS, BLOCKS), 0, 2 ** 20).astype(jnp.int32)
    scores = noise_bits * BLOCKS + blocks[None, None, :] + jnp.where(eligible, 0, 2 ** 30).astype(jnp.int32)
    chosen = jnp.argsort(scores, axis=-1, stable=True)[:, :, :SLOTS].astype(jnp.int32)
    return (pair_order, chosen, counts.astype(jnp.int32))


def draw_tile_cols(key, part):
    return fold_pattern(key)[1]


def draw_tile_counts(key, part):
    return fold_pattern(key)[2]


def draw_pair_order(key, part):
    return fold_pattern(key)[0]


def levels(key, shape, cuts, least, high):
    def one(axis_at, shards_of):
        steps = jax.random.uniform(jax.random.fold_in(jax.random.fold_in(key, 6), axis_at), (shards_of,), jnp.float32, least / len(cuts), high / len(cuts))
        return jnp.repeat(jnp.exp(steps), shape[axis_at] // shards_of).reshape((-1,) + (1,) * (len(shape) - axis_at - 1))

    loudness = one(*cuts[0])
    for cut in cuts[1:]:
        loudness = loudness * one(*cut)
    return loudness


def gaussian(own_key, dims, scale, reach, split=(), kind=jnp.bfloat16):
    drawn = jax.random.normal(own_key, dims, jnp.float32) * scale
    if len(split) > 0:
        drawn = levels(own_key, dims, split, -0.22, 0.18) * drawn
    return jnp.clip(drawn, min=-reach, max=reach).astype(kind)


def setup_inputs(seed: int = 0) -> dict:
    arg_keys = jax.random.split(jax.random.key(seed), 7)
    graph_tiles = gaussian(arg_keys[0], (BLOCKS, COLS, SLOTS, TILE, TILE), (TILE * SLOTS * N_COL * 3) ** -0.5, 0.0234375, ((0, 64), (1, 8)))
    tile_cols = draw_tile_cols(jax.random.fold_in(arg_keys[6], 71), 0)
    tile_counts = draw_tile_counts(jax.random.fold_in(arg_keys[6], 71), 0)
    pair_order = draw_pair_order(jax.random.fold_in(arg_keys[6], 71), 0)
    sketch = gaussian(arg_keys[4], (BLOCKS, TILE, RANK), 1.0, 6.0, ((0, 512),))
    degree_scale = jnp.clip(jnp.exp(math.log(2.5) - 1.8325814 * jax.random.uniform(arg_keys[5], (BLOCKS, TILE), jnp.float32) ** levels(arg_keys[5], (BLOCKS, TILE), ((0, 512),), -0.2, 0.2)), 0.4, 2.5)
    return dict(graph_tiles=graph_tiles, tile_cols=tile_cols, tile_counts=tile_counts, pair_order=pair_order, sketch=sketch, degree_scale=degree_scale)


EPSILON = 1e-05

def lower_solve(factor, rhs):
    return lax.linalg.triangular_solve(factor, rhs, left_side=True, lower=True)

def held_positions(pair_order):
    slot_of = jnp.zeros((PAIRS,), jnp.int32).at[pair_order].set(jnp.arange(PAIRS, dtype=jnp.int32))
    blocks = jnp.arange(BLOCKS, dtype=jnp.int32)
    lower_end = jnp.minimum(blocks, BLOCKS - 1 - blocks)
    return 2 * slot_of[lower_end] + (blocks >= PAIRS).astype(jnp.int32)

def reference(graph_tiles, tile_cols, tile_counts, pair_order, sketch, degree_scale):
    held_pos = held_positions(pair_order)
    targets = held_pos[tile_cols]
    live_mask = jnp.arange(SLOTS, dtype=jnp.int32)[None, None, :] < tile_counts[:, :, None]
    scaled = (degree_scale[:, :, None] * sketch.astype(jnp.float32)).astype(jnp.bfloat16)

    def row_step(totals, inputs):
        tile_row, target_row, live_row, own_rows = inputs
        masked = tile_row.astype(jnp.float32) * live_row[:, :, None, None].astype(jnp.float32)
        operands = scaled[target_row].astype(jnp.float32)
        forward = jnp.einsum('csab,csbk->ak', masked, operands)
        back_terms = jnp.einsum('csab,ak->csbk', masked, own_rows.astype(jnp.float32))
        totals = totals.at[target_row.reshape(-1)].add(back_terms.reshape(-1, TILE, RANK))
        return (totals, forward)
    start = jnp.zeros((BLOCKS, TILE, RANK), jnp.float32)
    transposed, forward = lax.scan(row_step, start, (graph_tiles, targets, live_mask, scaled))
    sketch_image = sketch.astype(jnp.float32) - degree_scale[:, :, None] * (forward + transposed)
    flat_image = sketch_image.reshape(-1, RANK)
    flat_sketch = sketch.astype(jnp.float32).reshape(-1, RANK)
    gram_sum = jnp.dot(flat_image.T, flat_image, precision=lax.Precision.HIGHEST) / NODES
    gram_sum = gram_sum + EPSILON * jnp.eye(RANK, dtype=jnp.float32)
    cross_raw = jnp.dot(flat_sketch.T, flat_image, precision=lax.Precision.HIGHEST) / NODES
    cross_sum = 0.5 * (cross_raw + cross_raw.T)
    factor = jnp.linalg.cholesky(gram_sum)
    sketch_basis = lower_solve(factor, flat_image.T).T.reshape(BLOCKS, TILE, RANK)
    half_way = lower_solve(factor, cross_sum)
    core_matrix = lower_solve(factor, half_way.T)
    return (sketch_basis, core_matrix)
```

```python
import jax
import jax.numpy as jnp
from jax import lax
from jax.experimental import pallas as pl
from jax.experimental.pallas import tpu as pltpu
from jax.sharding import Mesh, PartitionSpec as P

EPSILON = 1e-05
AXES = ("yh", "z", "core", "yl", "x")
SIZES = (2, 16, 2, 2, 4)
ROW = ("yh", "z", "core")
COL = ("yl", "x")
PLANE = ("yh", "core", "yl", "x")
GROUP = 4
VMEM_BYTES = 40 * 1024 * 1024
F32 = jnp.float32
BF16 = jnp.bfloat16


def exchange(array, axis):
    return lax.all_to_all(array, axis, 0, 0, tiled=True)


def spread(array, axis):
    count = lax.axis_size(axis)
    return exchange(jnp.broadcast_to(array[None], (count,) + array.shape), axis)


def swap(array, axis):
    return lax.ppermute(array, axis, [(0, 1), (1, 0)])


def full_dot(a, b, contract):
    return lax.dot_general(
        a, b, (contract, ((), ())), precision=lax.Precision.HIGHEST, preferred_element_type=F32
    )


def tile_copy(tiles_hbm, tiles, sems, q):
    return pltpu.make_async_copy(tiles_hbm.at[q, 0], tiles.at[q], sems.at[q])


def transposed_kernel(pos_ref, count_ref, own_ref, tiles_hbm, *rest):
    outs, (tiles, total, tile_sems, out_sems) = rest[:4], rest[4:]
    rows, slots = tiles.shape[0], tiles.shape[1]
    for q in range(rows):
        tile_copy(tiles_hbm, tiles, tile_sems, q).start()
    total[...] = jnp.zeros_like(total)

    def one_row(q, carry):
        tile_copy(tiles_hbm, tiles, tile_sems, q).wait()
        own = own_ref[q]
        count = count_ref[q]
        for first in range(0, slots, GROUP):
            group = range(first, min(first + GROUP, slots))

            @pl.when(count > first)
            def _(group=group):
                places = [pos_ref[q * slots + s] for s in group]
                terms = [
                    jnp.dot(own, tiles[q, s], preferred_element_type=F32) for s in group
                ]
                before = [total[p] for p in places]
                for p, old, term in zip(places, before, terms):
                    total[p] = old + term

        return carry

    lax.fori_loop(0, rows, one_row, 0)
    part = outs[0].shape[0]
    copies = [
        pltpu.make_async_copy(total.at[pl.ds(i * part, part)], out, out_sems.at[i])
        for i, out in enumerate(outs)
    ]
    for copy in copies:
        copy.start()
    for copy in copies:
        copy.wait()


def forward_kernel(pos_ref, count_ref, *rest):
    parts, (tiles_hbm, out_ref, tiles, blocks, total, tile_sems, part_sems) = rest[:4], rest[4:]
    rows, slots = tiles.shape[0], tiles.shape[1]
    part = parts[0].shape[0]
    copies = [
        pltpu.make_async_copy(ref, blocks.at[pl.ds(i * part, part)], part_sems.at[i])
        for i, ref in enumerate(parts)
    ]
    for copy in copies:
        copy.start()
    for q in range(rows):
        tile_copy(tiles_hbm, tiles, tile_sems, q).start()
    blocks[len(parts) * part] = jnp.zeros(blocks.shape[1:], blocks.dtype)
    for copy in copies:
        copy.wait()

    def one_row(q, carry):
        tile_copy(tiles_hbm, tiles, tile_sems, q).wait()
        count = count_ref[q]
        total[...] = jnp.zeros_like(total)
        for first in range(0, slots, GROUP):
            group = range(first, min(first + GROUP, slots))

            @pl.when(count > first)
            def _(group=group):
                left = jnp.concatenate([tiles[q, s] for s in group], axis=1)
                right = jnp.concatenate([blocks[pos_ref[q * slots + s]] for s in group], axis=0)
                total[...] += jnp.dot(left, right, preferred_element_type=F32)

        out_ref[q] = total[...].astype(out_ref.dtype)
        return carry

    lax.fori_loop(0, rows, one_row, 0)


def image_kernel(back_ref, fore_ref, sketch_ref, scale_ref, image_ref, sums_ref):
    back = back_ref[0].astype(F32)
    for i in range(1, back_ref.shape[0]):
        back = back + back_ref[i].astype(F32)
    fore = fore_ref[0].astype(F32)
    for i in range(1, fore_ref.shape[0]):
        fore = fore + fore_ref[i].astype(F32)
    sketch = sketch_ref[...].astype(F32)
    scale = jnp.broadcast_to(scale_ref[...], sketch.shape).T
    image = sketch - scale * (fore + back.T)
    image_ref[...] = image
    width = image.shape[1]
    sums_ref[0:width, :] = full_dot(image, image, ((0,), (0,)))
    sums_ref[width:, :] = full_dot(sketch, image, ((0,), (0,)))


def whiten_kernel(node_count, sums_ref, image_ref, basis_ref, core_ref):
    width = image_ref.shape[1]
    line = lax.broadcasted_iota(jnp.int32, (width, width), 0)
    lane = lax.broadcasted_iota(jnp.int32, (width, width), 1)
    eye = jnp.where(line == lane, 1.0, 0.0).astype(F32)
    gram = sums_ref[0:width, :] / node_count + EPSILON * eye
    cross = sums_ref[width:, :] / node_count
    cross = 0.5 * (cross + cross.T)
    step = 8
    bands = width // step
    left = [gram[step * k : step * (k + 1), :] for k in range(bands)]
    right = [eye[step * k : step * (k + 1), :] for k in range(bands)]
    sub = lax.broadcasted_iota(jnp.int32, (step, width), 0)
    pivots = [jnp.ones((step, width), F32) for _ in range(bands)]
    for j in range(width):
        at, i = divmod(j, step)
        columns = [None] * bands
        for k in range(at, bands):
            columns[k] = jnp.broadcast_to(left[k][:, j : j + 1], (step, width))
        pivot = jnp.broadcast_to(columns[at][i : i + 1, :], (step, width))
        inverse = 1.0 / pivot
        pivots[at] = jnp.where(sub == i, pivot, pivots[at])
        row_left = jnp.broadcast_to(left[at][i : i + 1, :], (step, width)) * inverse
        row_right = jnp.broadcast_to(right[at][i : i + 1, :], (step, width)) * inverse
        columns[at] = jnp.where(sub > i, columns[at], 0.0)
        for k in range(at, bands):
            left[k] = left[k] - columns[k] * row_left
            right[k] = right[k] - columns[k] * row_right
    whitener = jnp.concatenate([r * lax.rsqrt(p) for r, p in zip(right, pivots)], axis=0)
    basis_ref[...] = full_dot(image_ref[...], whitener, ((1,), (1,)))
    half_way = full_dot(whitener, cross, ((1,), (0,)))
    core_ref[...] = full_dot(half_way, whitener, ((1,), (1,)))


def spec(space):
    return pl.BlockSpec(memory_space=space)


def call(kernel, out_shape, in_spaces, out_spaces, scratch, name):
    many = isinstance(out_spaces, tuple)
    return pl.pallas_call(
        kernel,
        out_shape=out_shape,
        in_specs=[spec(s) for s in in_spaces],
        out_specs=tuple(spec(s) for s in out_spaces) if many else spec(out_spaces),
        scratch_shapes=scratch,
        compiler_params=pltpu.CompilerParams(vmem_limit_bytes=VMEM_BYTES),
        name=name,
    )


def body(graph_tiles, tile_cols, tile_counts, pair_order, sketch, degree_scale):
    rows, _, slots, width, _ = graph_tiles.shape
    rank = sketch.shape[2]
    pairs = pair_order.shape[0]
    node_count = 2 * pairs * width
    z_count = lax.axis_size("z")
    col_count = lax.axis_size(COL)
    ANY, VMEM, SMEM = pl.ANY, pltpu.VMEM, pltpu.SMEM

    scaled = (degree_scale[:, :, None] * sketch.astype(F32)).astype(BF16)[0]

    natural = tile_cols[:, 0, :]
    lower_end = jnp.minimum(natural, 2 * pairs - 1 - natural)
    hit = lower_end[:, :, None] == pair_order[None, None, :]
    pair_slot = jnp.sum(jnp.where(hit, jnp.arange(pairs, dtype=jnp.int32), 0), axis=-1)
    held = 2 * pair_slot + (natural >= pairs).astype(jnp.int32)
    owner = held // col_count
    other_core = (owner % 2) ^ lax.axis_index("core")
    other_half = (owner // (2 * z_count)) ^ lax.axis_index("yh")
    place = (other_core * 2 + other_half) * z_count + owner // 2 % z_count
    counts = tile_counts[:, 0]
    live = jnp.arange(slots, dtype=jnp.int32)[None, :] < counts[:, None]
    place = jnp.where(live, place, 4 * z_count).reshape(-1)

    tile_scratch = pltpu.VMEM((rows, slots, width, width), BF16)
    part = jax.ShapeDtypeStruct((z_count, rank, width), F32)

    own_rows = spread(scaled.T, COL)
    keep0, keep1, send0, send1 = call(
        transposed_kernel,
        (part,) * 4,
        (SMEM, SMEM, VMEM, ANY),
        (ANY,) * 4,
        [
            tile_scratch,
            pltpu.VMEM((4 * z_count + 1, rank, width), F32),
            pltpu.SemaphoreType.DMA((rows,)),
            pltpu.SemaphoreType.DMA((4,)),
        ],
        "transposed_products",
    )(place, counts, own_rows, graph_tiles)
    far = (keep1 + swap(send1, "core")).astype(BF16)
    near = swap(send0, "core")
    far = swap(far, "yh")
    scaled, far = lax.optimization_barrier((scaled, far))
    gather0 = lax.all_gather(scaled, "z")
    gather1 = swap(gather0, "yh")
    gather2 = swap(gather0, "core")
    gather3 = swap(gather1, "core")
    back = exchange((keep0 + near + far.astype(F32)).astype(BF16), "z")
    forward = call(
        forward_kernel,
        jax.ShapeDtypeStruct((rows, width, rank), BF16),
        (SMEM, SMEM) + (ANY,) * 5,
        VMEM,
        [
            tile_scratch,
            pltpu.VMEM((4 * z_count + 1, width, rank), BF16),
            pltpu.VMEM((width, rank), F32),
            pltpu.SemaphoreType.DMA((rows,)),
            pltpu.SemaphoreType.DMA((4,)),
        ],
        "forward_products",
    )(place, counts, gather0, gather1, gather2, gather3, graph_tiles)
    fore = exchange(forward, COL)

    image, sums = call(
        image_kernel,
        (jax.ShapeDtypeStruct((width, rank), F32), jax.ShapeDtypeStruct((2 * rank, rank), F32)),
        (VMEM,) * 4,
        (VMEM,) * 2,
        [],
        "image_and_grams",
    )(back, fore, sketch[0], degree_scale)

    pieces = lax.axis_size(PLANE)
    sums = exchange(sums.reshape(pieces, 2 * rank // pieces, rank), PLANE).sum(axis=0)
    sums = spread(sums, "z").sum(axis=0)
    sums = spread(sums, PLANE).reshape(2 * rank, rank)

    def whiten(*refs):
        whiten_kernel(node_count, *refs)

    basis, core_matrix = call(
        whiten,
        (jax.ShapeDtypeStruct((width, rank), F32), jax.ShapeDtypeStruct((rank, rank), F32)),
        (VMEM,) * 2,
        (VMEM,) * 2,
        [],
        "whiten",
    )(sums, image)
    return basis[None], core_matrix


def solution(mesh):
    fine = Mesh(mesh.devices.reshape(SIZES), AXES)
    return jax.shard_map(
        body,
        mesh=fine,
        in_specs=(
            P(ROW, COL, None, None, None),
            P(ROW, COL, None),
            P(ROW, COL),
            P(),
            P(AXES, None, None),
            P(AXES, None),
        ),
        out_specs=(P(AXES, None, None), P()),
        check_vma=False,
    )
```

```python
import jax
import jax.numpy as jnp
from jax import lax
from jax.experimental import pallas as pl
from jax.experimental.pallas import tpu as pltpu
from jax.sharding import Mesh, PartitionSpec as P

EPSILON = 1e-05
AXES = ("yh", "z", "core", "yl", "x")
SIZES = (2, 16, 2, 2, 4)
ROW = ("yh", "z", "core")
COL = ("yl", "x")
PLANE = ("yh", "core", "yl", "x")
GROUP = 19
NO_COST = pl.CostEstimate(flops=0, bytes_accessed=0, transcendentals=0)
VMEM_BYTES = 57 * 1024 * 1024
F32 = jnp.float32
BF16 = jnp.bfloat16


def exchange(array, axis):
    return lax.all_to_all(array, axis, 0, 0, tiled=True)


def spread(array, axis):
    return exchange(jnp.broadcast_to(array[None], (lax.axis_size(axis),) + array.shape), axis)


def swap(array, axis):
    return lax.ppermute(array, axis, [(0, 1), (1, 0)])


def after(array, *others):
    return lax.optimization_barrier((array, *others))[0]


def full_dot(a, b, contract):
    return lax.dot_general(
        a, b, (contract, ((), ())), precision=lax.Precision.HIGHEST, preferred_element_type=F32
    )


def tile_copy(tiles_hbm, tiles, sems, q):
    return pltpu.make_async_copy(tiles_hbm.at[q, 0], tiles.at[q], sems.at[q])


def place_kernel(order_ref, cols_ref, count_ref, place_ref, slot_of):
    rows, slots = cols_ref.shape
    pairs = order_ref.shape[0]
    core, half = lax.axis_index("core"), lax.axis_index("yh")

    def one_pair(p, carry):
        slot_of[order_ref[p]] = p
        return carry

    lax.fori_loop(0, pairs, one_pair, 0, unroll=16)

    def one_row(q, carry):
        count = count_ref[q, 0]
        for s in range(slots):
            natural = cols_ref[q, s]
            upper = natural >= pairs
            slot = slot_of[jnp.where(upper, 2 * pairs - 1 - natural, natural)]
            owner = lax.shift_right_logical(2 * slot + upper.astype(jnp.int32), 3)
            side = 2 * ((owner & 1) ^ core) + ((lax.shift_right_logical(owner, 5) & 1) ^ half)
            place = side * 16 + (lax.shift_right_logical(owner, 1) & 15)
            place_ref[q * slots + s] = jnp.where(s < count, place, 64)
        return carry

    lax.fori_loop(0, rows, one_row, 0)


def scale_kernel(sketch_ref, scale_ref, own_ref, gather_ref):
    sketch = sketch_ref[...].astype(F32)
    scaled = jnp.broadcast_to(scale_ref[...], sketch.shape).T * sketch
    turned, scaled = scaled.T.astype(BF16), scaled.astype(BF16)
    for i in range(own_ref.shape[0]):
        own_ref[i] = turned
    for i in range(gather_ref.shape[0]):
        gather_ref[i] = scaled


def transposed_kernel(pos_ref, count_ref, own_hbm, tiles_hbm, *rest):
    outs, (own_ref, tiles, total, own_sem, tile_sems, out_sems) = rest[:4], rest[4:]
    rows, slots = tiles.shape[0], tiles.shape[1]
    z_count = outs[0].shape[0]
    own_copy = pltpu.make_async_copy(own_hbm, own_ref, own_sem)
    own_copy.start()
    for q in range(rows):
        tile_copy(tiles_hbm, tiles, tile_sems, q).start()
    total[...] = jnp.zeros_like(total)
    own_copy.wait()

    def one_row(q, carry):
        tile_copy(tiles_hbm, tiles, tile_sems, q).wait()
        own = own_ref[q]
        count = count_ref[q, 0]
        for first in range(0, slots, GROUP):
            group = range(first, min(first + GROUP, slots))

            @pl.when(count > first)
            def _(group=group):
                places = [pos_ref[q * slots + s] for s in group]
                terms = [jnp.dot(own, tiles[q, s], preferred_element_type=F32) for s in group]
                before = [total[p] for p in places]
                for p, old, term in zip(places, before, terms):
                    total[p] = old + term

        return carry

    lax.fori_loop(0, rows, one_row, 0)
    copies = [
        pltpu.make_async_copy(total.at[pl.ds(i * z_count, z_count)], out, out_sems.at[i])
        for i, out in enumerate(outs)
    ]
    for copy in copies:
        copy.start()
    for copy in copies:
        copy.wait()


def forward_kernel(pos_ref, count_ref, *rest):
    parts, (tiles_hbm, out_ref, tiles, blocks, total, tile_sems, part_sems) = rest[:4], rest[4:]
    rows, slots = tiles.shape[0], tiles.shape[1]
    part = parts[0].shape[0]
    copies = [
        pltpu.make_async_copy(ref, blocks.at[pl.ds(i * part, part)], part_sems.at[i])
        for i, ref in enumerate(parts)
    ]
    for copy in copies:
        copy.start()
    ahead = 3
    for q in range(ahead):
        tile_copy(tiles_hbm, tiles, tile_sems, q).start()
    blocks[4 * part] = jnp.zeros(blocks.shape[1:], blocks.dtype)
    for copy in copies:
        copy.wait()

    def one_row(q, carry):
        tile_copy(tiles_hbm, tiles, tile_sems, q).wait()

        @pl.when(q + ahead < rows)
        def _():
            tile_copy(tiles_hbm, tiles, tile_sems, q + ahead).start()

        count = count_ref[q, 0]
        total[...] = jnp.zeros_like(total)
        for first in range(0, slots, GROUP):
            group = range(first, min(first + GROUP, slots))

            @pl.when(count > first)
            def _(group=group):
                left = jnp.concatenate([tiles[q, s] for s in group], axis=1)
                right = jnp.concatenate([blocks[pos_ref[q * slots + s]] for s in group], axis=0)
                total[...] += jnp.dot(left, right, preferred_element_type=F32)

        out_ref[q] = total[...].astype(out_ref.dtype)
        return carry

    lax.fori_loop(0, rows, one_row, 0)


def image_kernel(back_ref, fore_ref, sketch_ref, scale_ref, image_ref, sums_ref):
    back = back_ref[...]
    fore = fore_ref[0].astype(F32)
    for i in range(1, fore_ref.shape[0]):
        fore = fore + fore_ref[i].astype(F32)
    sketch = sketch_ref[...].astype(F32)
    scale = jnp.broadcast_to(scale_ref[...], sketch.shape).T
    image = sketch - scale * (fore + back.T)
    image_ref[...] = image
    width = image.shape[1]
    sums_ref[0:width, :] = full_dot(image, image, ((0,), (0,)))
    sums_ref[width:, :] = full_dot(sketch, image, ((0,), (0,)))


def whiten_kernel(node_count, sums_ref, image_ref, basis_ref, core_ref):
    width = image_ref.shape[1]
    line = lax.broadcasted_iota(jnp.int32, (width, width), 0)
    lane = lax.broadcasted_iota(jnp.int32, (width, width), 1)
    eye = jnp.where(line == lane, 1.0, 0.0).astype(F32)
    gram = sums_ref[0:width, :] / node_count + EPSILON * eye
    cross = sums_ref[width:, :] / node_count
    cross = 0.5 * (cross + cross.T)
    step = 8
    bands = width // step
    left = [gram[step * k : step * (k + 1), :] for k in range(bands)]
    right = [eye[step * k : step * (k + 1), :] for k in range(bands)]
    sub = lax.broadcasted_iota(jnp.int32, (step, width), 0)

    def line_of(band, i):
        return jnp.broadcast_to(band[i : i + 1, :], (step, width))

    def lane_of(band, j):
        return jnp.broadcast_to(band[:, j : j + 1], (step, width))

    whitener = []
    for at in range(bands):
        first = step * at
        lanes = [lane_of(left[at], first + i) for i in range(step)]
        block = [[line_of(lanes[j], i) for j in range(i + 1)] for i in range(step)]
        lower = [[None] * step for _ in range(step)]
        inverse = []
        for j in range(step):
            inverse.append(1.0 / block[j][j])
            for i in range(j + 1, step):
                lower[i][j] = block[i][j] * inverse[j]
            for i in range(j + 1, step):
                for k in range(j + 1, i + 1):
                    block[i][k] = block[i][k] - lower[i][j] * block[k][j]
        solved = []
        for band in (left[at], right[at]):
            lines = [line_of(band, i) for i in range(step)]
            for j in range(step):
                for i in range(j + 1, step):
                    lines[i] = lines[i] - lower[i][j] * lines[j]
            solved.append(lines)
        scaled = jnp.zeros((step, width), F32)
        for i in range(step):
            scaled = jnp.where(sub == i, solved[1][i] * lax.rsqrt(block[i][i]), scaled)
        whitener.append(scaled)
        if at + 1 == bands:
            break
        for lines in solved:
            for i in range(step):
                lines[i] = lines[i] * inverse[i]
            for j in reversed(range(step)):
                for i in range(j):
                    lines[i] = lines[i] - lower[j][i] * lines[j]
        for k in range(at + 1, bands):
            lanes = [lane_of(left[k], first + i) for i in range(step)]
            for i in range(step):
                left[k] = left[k] - lanes[i] * solved[0][i]
                right[k] = right[k] - lanes[i] * solved[1][i]
    whitener = jnp.concatenate(whitener, axis=0)
    basis_ref[...] = full_dot(image_ref[...], whitener, ((1,), (1,)))
    half_way = full_dot(whitener, cross, ((1,), (0,)))
    core_ref[...] = full_dot(half_way, whitener, ((1,), (1,)))


def spec(space):
    return pl.BlockSpec(memory_space=space)


def call(kernel, out_shape, in_spaces, out_spaces, scratch, name, cost=NO_COST):
    many = isinstance(out_spaces, tuple)
    return pl.pallas_call(
        kernel,
        out_shape=out_shape,
        in_specs=[spec(s) for s in in_spaces],
        out_specs=tuple(spec(s) for s in out_spaces) if many else spec(out_spaces),
        scratch_shapes=scratch,
        compiler_params=pltpu.CompilerParams(vmem_limit_bytes=VMEM_BYTES),
        cost_estimate=cost,
        name=name,
    )


def body(graph_tiles, tile_cols, tile_counts, pair_order, sketch, degree_scale):
    rows, _, slots, width, _ = graph_tiles.shape
    rank = sketch.shape[2]
    pairs = pair_order.shape[0]
    node_count = 2 * pairs * width
    z_count = lax.axis_size("z")
    HBM, VMEM, SMEM = pltpu.HBM, pltpu.VMEM, pltpu.SMEM

    own_rows, gather = call(
        scale_kernel,
        (
            jax.ShapeDtypeStruct((lax.axis_size(COL), rank, width), BF16),
            jax.ShapeDtypeStruct((z_count, width, rank), BF16),
        ),
        (VMEM,) * 2,
        (VMEM,) * 2,
        [],
        "scale",
    )(sketch[0], degree_scale)
    tile_scratch = pltpu.VMEM((rows, slots, width, width), BF16)
    row_sems = pltpu.SemaphoreType.DMA((rows,))
    part_sems = pltpu.SemaphoreType.DMA((4,))
    part = jax.ShapeDtypeStruct((z_count, rank, width), F32)

    places = call(
        place_kernel,
        jax.ShapeDtypeStruct((rows * slots,), jnp.int32),
        (SMEM, SMEM, SMEM),
        SMEM,
        [pltpu.SMEM((pairs,), jnp.int32)],
        "places",
    )(pair_order, tile_cols[:, 0, :], tile_counts)
    own_rows = exchange(own_rows, COL)
    gather = exchange(after(gather, places), "z")
    near, far, near_send, far_send = call(
        transposed_kernel,
        (part,) * 4,
        (SMEM, SMEM, HBM, HBM),
        (HBM,) * 4,
        [
            pltpu.VMEM((rows, rank, width), BF16),
            tile_scratch,
            pltpu.VMEM((4 * z_count + 1, rank, width), F32),
            pltpu.SemaphoreType.DMA,
            row_sems,
            part_sems,
        ],
        "transposed_products",
    )(places, tile_counts, own_rows, graph_tiles)
    far_got = swap(far_send, "core")
    near_got = swap(near_send, "core")
    far = (far + far_got).astype(BF16)
    near = lax.optimization_barrier(near + near_got)
    back = (near + swap(far, "yh").astype(F32)).astype(BF16)
    gather = after(gather, far, near_got)
    gather1 = after(swap(gather, "yh"), back)
    gather2 = swap(gather, "core")
    gather3 = swap(gather1, "core")
    back = exchange(back, "z")
    forward = call(
        forward_kernel,
        jax.ShapeDtypeStruct((rows, width, rank), BF16),
        (SMEM, SMEM) + (HBM,) * 5,
        VMEM,
        [
            tile_scratch,
            pltpu.VMEM((4 * z_count + 1, width, rank), BF16),
            pltpu.VMEM((width, rank), F32),
            row_sems,
            part_sems,
        ],
        "forward_products",
        pl.CostEstimate(flops=12650000000, bytes_accessed=0, transcendentals=0),
    )(places, tile_counts, gather, gather1, gather2, gather3, graph_tiles)
    fore = exchange(after(forward, back), COL)
    back = back.astype(F32).sum(axis=0)

    image, sums = call(
        image_kernel,
        (jax.ShapeDtypeStruct((width, rank), F32), jax.ShapeDtypeStruct((2 * rank, rank), F32)),
        (VMEM,) * 4,
        (VMEM,) * 2,
        [],
        "image_and_grams",
    )(back, fore, sketch[0], degree_scale)

    pieces = lax.axis_size(PLANE)
    sums = exchange(sums.reshape(pieces, 2 * rank // pieces, rank), PLANE).sum(axis=0)
    sums = spread(sums, "z").sum(axis=0)
    sums = spread(sums, PLANE).reshape(2 * rank, rank)

    def whiten(*refs):
        whiten_kernel(node_count, *refs)

    basis, core_matrix = call(
        whiten,
        (jax.ShapeDtypeStruct((width, rank), F32), jax.ShapeDtypeStruct((rank, rank), F32)),
        (VMEM,) * 2,
        (VMEM,) * 2,
        [],
        "whiten",
    )(sums, image)
    return basis[None], core_matrix


def solution(mesh):
    fine = Mesh(mesh.devices.reshape(SIZES), AXES)
    return jax.shard_map(
        body,
        mesh=fine,
        in_specs=(
            P(ROW, COL, None, None, None),
            P(ROW, COL, None),
            P(ROW, COL),
            P(),
            P(AXES, None, None),
            P(AXES, None),
        ),
        out_specs=(P(AXES, None, None), P()),
        check_vma=False,
    )
```

```python
import jax
import jax.numpy as jnp
from jax import lax
from jax.experimental import pallas as pl
from jax.experimental.pallas import tpu as pltpu
from jax.sharding import Mesh, PartitionSpec as P

EPSILON = 1e-05
AXES = ("yh", "z", "core", "yl", "x")
SIZES = (2, 16, 2, 2, 4)
ROW = ("yh", "z", "core")
COL = ("yl", "x")
PLANE = ("yh", "core", "yl", "x")
GROUP = 19
NO_COST = pl.CostEstimate(flops=0, bytes_accessed=0, transcendentals=0)
VMEM_BYTES = 16 * 1024 * 1024
TILE_VMEM_BYTES = 50 * 1024 * 1024
F32 = jnp.float32
BF16 = jnp.bfloat16


def exchange(array, axis):
    return lax.all_to_all(array, axis, 0, 0, tiled=True)


def spread(array, axis):
    return exchange(jnp.broadcast_to(array[None], (lax.axis_size(axis),) + array.shape), axis)


def swap(array, axis):
    return lax.ppermute(array, axis, [(0, 1), (1, 0)])


def after(array, *others):
    return lax.optimization_barrier((array, *others))[0]


def full_dot(a, b, contract):
    return lax.dot_general(
        a, b, (contract, ((), ())), precision=lax.Precision.HIGHEST, preferred_element_type=F32
    )


def tile_copy(tiles_hbm, tiles, sems, q):
    return pltpu.make_async_copy(tiles_hbm.at[q, 0], tiles.at[q], sems.at[q])


def place_kernel(order_ref, cols_ref, count_ref, place_ref, slot_of):
    rows, slots = cols_ref.shape
    pairs = order_ref.shape[0]
    core, half = lax.axis_index("core"), lax.axis_index("yh")

    def one_pair(p, carry):
        slot_of[order_ref[p]] = p
        return carry

    lax.fori_loop(0, pairs, one_pair, 0, unroll=16)

    def one_row(q, carry):
        count = count_ref[q, 0]
        for s in range(slots):
            natural = cols_ref[q, s]
            upper = natural >= pairs
            slot = slot_of[jnp.where(upper, 2 * pairs - 1 - natural, natural)]
            owner = lax.shift_right_logical(2 * slot + upper.astype(jnp.int32), 3)
            side = 2 * ((owner & 1) ^ core) + ((lax.shift_right_logical(owner, 5) & 1) ^ half)
            place = side * 16 + (lax.shift_right_logical(owner, 1) & 15)
            place_ref[q * slots + s] = jnp.where(s < count, place, 64)
        return carry

    lax.fori_loop(0, rows, one_row, 0)


def scale_kernel(sketch_ref, scale_ref, own_ref, gather_ref):
    sketch = sketch_ref[...].astype(F32)
    scaled = jnp.broadcast_to(scale_ref[...], sketch.shape).T * sketch
    turned, scaled = scaled.T.astype(BF16), scaled.astype(BF16)
    for i in range(own_ref.shape[0]):
        own_ref[i] = turned
    for i in range(gather_ref.shape[0]):
        gather_ref[i] = scaled


def transposed_kernel(pos_ref, count_ref, own_hbm, tiles_hbm, *rest):
    outs, (own_ref, tiles, total, own_sem, tile_sems, out_sems) = rest[:4], rest[4:]
    rows, slots = tiles.shape[0], tiles.shape[1]
    z_count = outs[0].shape[0]
    own_copy = pltpu.make_async_copy(own_hbm, own_ref, own_sem)
    own_copy.start()
    for q in range(rows):
        tile_copy(tiles_hbm, tiles, tile_sems, q).start()
    total[...] = jnp.zeros_like(total)
    own_copy.wait()

    def one_row(q, carry):
        tile_copy(tiles_hbm, tiles, tile_sems, q).wait()
        own = own_ref[q]
        count = count_ref[q, 0]
        for first in range(0, slots, GROUP):
            group = range(first, min(first + GROUP, slots))

            @pl.when(count > first)
            def _(group=group):
                places = [pos_ref[q * slots + s] for s in group]
                terms = [jnp.dot(own, tiles[q, s], preferred_element_type=F32) for s in group]
                before = [total[p] for p in places]
                for p, old, term in zip(places, before, terms):
                    total[p] = old + term

        return carry

    lax.fori_loop(0, rows, one_row, 0)
    copies = [
        pltpu.make_async_copy(total.at[pl.ds(i * z_count, z_count)], out, out_sems.at[i])
        for i, out in enumerate(outs)
    ]
    for copy in copies:
        copy.start()
    for copy in copies:
        copy.wait()


def forward_kernel(pos_ref, count_ref, *rest):
    parts, (tiles_hbm, out_ref, tiles, blocks, total, tile_sems, part_sems) = rest[:4], rest[4:]
    rows, slots = tiles.shape[0], tiles.shape[1]
    part = parts[0].shape[0]
    copies = [
        pltpu.make_async_copy(ref, blocks.at[pl.ds(i * part, part)], part_sems.at[i])
        for i, ref in enumerate(parts)
    ]
    for copy in copies:
        copy.start()
    ahead = 3
    for q in range(ahead):
        tile_copy(tiles_hbm, tiles, tile_sems, q).start()
    blocks[4 * part] = jnp.zeros(blocks.shape[1:], blocks.dtype)
    for copy in copies:
        copy.wait()

    def one_row(q, carry):
        tile_copy(tiles_hbm, tiles, tile_sems, q).wait()

        @pl.when(q + ahead < rows)
        def _():
            tile_copy(tiles_hbm, tiles, tile_sems, q + ahead).start()

        count = count_ref[q, 0]
        total[...] = jnp.zeros_like(total)
        for first in range(0, slots, GROUP):
            group = range(first, min(first + GROUP, slots))

            @pl.when(count > first)
            def _(group=group):
                left = jnp.concatenate([tiles[q, s] for s in group], axis=1)
                right = jnp.concatenate([blocks[pos_ref[q * slots + s]] for s in group], axis=0)
                total[...] += jnp.dot(left, right, preferred_element_type=F32)

        out_ref[q] = total[...].astype(out_ref.dtype)
        return carry

    lax.fori_loop(0, rows, one_row, 0)


def image_kernel(back_ref, fore_ref, sketch_ref, scale_ref, image_ref, sums_ref):
    back = back_ref[...]
    fore = fore_ref[0].astype(F32)
    for i in range(1, fore_ref.shape[0]):
        fore = fore + fore_ref[i].astype(F32)
    sketch = sketch_ref[...].astype(F32)
    scale = jnp.broadcast_to(scale_ref[...], sketch.shape).T
    image = sketch - scale * (fore + back.T)
    image_ref[...] = image
    width = image.shape[1]
    sums_ref[0:width, :] = full_dot(image, image, ((0,), (0,)))
    sums_ref[width:, :] = full_dot(sketch, image, ((0,), (0,)))


def whiten_kernel(node_count, sums_ref, image_ref, basis_ref, core_ref):
    width = image_ref.shape[1]
    line = lax.broadcasted_iota(jnp.int32, (width, width), 0)
    lane = lax.broadcasted_iota(jnp.int32, (width, width), 1)
    eye = jnp.where(line == lane, 1.0, 0.0).astype(F32)
    gram = sums_ref[0:width, :] / node_count + EPSILON * eye
    cross = sums_ref[width:, :] / node_count
    cross = 0.5 * (cross + cross.T)
    step = 8
    bands = width // step
    left = [gram[step * k : step * (k + 1), :] for k in range(bands)]
    right = [eye[step * k : step * (k + 1), :] for k in range(bands)]
    sub = lax.broadcasted_iota(jnp.int32, (step, width), 0)

    def line_of(band, i):
        return jnp.broadcast_to(band[i : i + 1, :], (step, width))

    def lane_of(band, j):
        return jnp.broadcast_to(band[:, j : j + 1], (step, width))

    whitener = []
    for at in range(bands):
        first = step * at
        lanes = [lane_of(left[at], first + i) for i in range(step)]
        block = [[line_of(lanes[j], i) for j in range(i + 1)] for i in range(step)]
        lower = [[None] * step for _ in range(step)]
        inverse = []
        for j in range(step):
            inverse.append(1.0 / block[j][j])
            for i in range(j + 1, step):
                lower[i][j] = block[i][j] * inverse[j]
            for i in range(j + 1, step):
                for k in range(j + 1, i + 1):
                    block[i][k] = block[i][k] - lower[i][j] * block[k][j]
        solved = []
        for band in (left[at], right[at]):
            lines = [line_of(band, i) for i in range(step)]
            for j in range(step):
                for i in range(j + 1, step):
                    lines[i] = lines[i] - lower[i][j] * lines[j]
            solved.append(lines)
        scaled = jnp.zeros((step, width), F32)
        for i in range(step):
            scaled = jnp.where(sub == i, solved[1][i] * lax.rsqrt(block[i][i]), scaled)
        whitener.append(scaled)
        if at + 1 == bands:
            break
        for lines in solved:
            for i in range(step):
                lines[i] = lines[i] * inverse[i]
            for j in reversed(range(step)):
                for i in range(j):
                    lines[i] = lines[i] - lower[j][i] * lines[j]
        for k in range(at + 1, bands):
            lanes = [lane_of(left[k], first + i) for i in range(step)]
            for i in range(step):
                left[k] = left[k] - lanes[i] * solved[0][i]
                right[k] = right[k] - lanes[i] * solved[1][i]
    whitener = jnp.concatenate(whitener, axis=0)
    basis_ref[...] = full_dot(image_ref[...], whitener, ((1,), (1,)))
    half_way = full_dot(whitener, cross, ((1,), (0,)))
    core_ref[...] = full_dot(half_way, whitener, ((1,), (1,)))


def spec(space):
    return pl.BlockSpec(memory_space=space)


def call(kernel, out_shape, in_spaces, out_spaces, scratch, name, cost=NO_COST, vmem=VMEM_BYTES):
    many = isinstance(out_spaces, tuple)
    return pl.pallas_call(
        kernel,
        out_shape=out_shape,
        in_specs=[spec(s) for s in in_spaces],
        out_specs=tuple(spec(s) for s in out_spaces) if many else spec(out_spaces),
        scratch_shapes=scratch,
        compiler_params=pltpu.CompilerParams(vmem_limit_bytes=vmem),
        cost_estimate=cost,
        name=name,
    )


def body(graph_tiles, tile_cols, tile_counts, pair_order, sketch, degree_scale):
    rows, _, slots, width, _ = graph_tiles.shape
    rank = sketch.shape[2]
    pairs = pair_order.shape[0]
    node_count = 2 * pairs * width
    z_count = lax.axis_size("z")
    HBM, VMEM, SMEM = pltpu.HBM, pltpu.VMEM, pltpu.SMEM

    own_rows, gather = call(
        scale_kernel,
        (
            jax.ShapeDtypeStruct((lax.axis_size(COL), rank, width), BF16),
            jax.ShapeDtypeStruct((z_count, width, rank), BF16),
        ),
        (VMEM,) * 2,
        (VMEM,) * 2,
        [],
        "scale",
    )(sketch[0], degree_scale)
    tile_scratch = pltpu.VMEM((rows, slots, width, width), BF16)
    row_sems = pltpu.SemaphoreType.DMA((rows,))
    part_sems = pltpu.SemaphoreType.DMA((4,))
    part = jax.ShapeDtypeStruct((z_count, rank, width), F32)

    places = call(
        place_kernel,
        jax.ShapeDtypeStruct((rows * slots,), jnp.int32),
        (SMEM, SMEM, SMEM),
        SMEM,
        [pltpu.SMEM((pairs,), jnp.int32)],
        "places",
    )(pair_order, tile_cols[:, 0, :], tile_counts)
    own_rows = exchange(own_rows, COL)
    gather = exchange(after(gather, places), "z")
    near, far, near_send, far_send = call(
        transposed_kernel,
        (part,) * 4,
        (SMEM, SMEM, HBM, HBM),
        (HBM,) * 4,
        [
            pltpu.VMEM((rows, rank, width), BF16),
            tile_scratch,
            pltpu.VMEM((4 * z_count + 1, rank, width), F32),
            pltpu.SemaphoreType.DMA,
            row_sems,
            part_sems,
        ],
        "transposed_products",
        vmem=TILE_VMEM_BYTES,
    )(places, tile_counts, own_rows, graph_tiles)
    far_got = swap(far_send, "core")
    near_got = swap(near_send, "core")
    far = (far + far_got).astype(BF16)
    near = lax.optimization_barrier(near + near_got)
    back = (near + swap(far, "yh").astype(F32)).astype(BF16)
    gather = after(gather, far, near_got)
    gather1 = after(swap(gather, "yh"), back)
    gather2 = swap(gather, "core")
    gather3 = swap(gather1, "core")
    back = exchange(back, "z")
    forward = call(
        forward_kernel,
        jax.ShapeDtypeStruct((rows, width, rank), BF16),
        (SMEM, SMEM) + (HBM,) * 5,
        VMEM,
        [
            tile_scratch,
            pltpu.VMEM((4 * z_count + 1, width, rank), BF16),
            pltpu.VMEM((width, rank), F32),
            row_sems,
            part_sems,
        ],
        "forward_products",
        pl.CostEstimate(flops=12650000000, bytes_accessed=0, transcendentals=0),
        TILE_VMEM_BYTES,
    )(places, tile_counts, gather, gather1, gather2, gather3, graph_tiles)
    fore = exchange(after(forward, back), COL)
    back = back.astype(F32).sum(axis=0)

    image, sums = call(
        image_kernel,
        (jax.ShapeDtypeStruct((width, rank), F32), jax.ShapeDtypeStruct((2 * rank, rank), F32)),
        (VMEM,) * 4,
        (VMEM,) * 2,
        [],
        "image_and_grams",
    )(back, fore, sketch[0], degree_scale)

    pieces = lax.axis_size(PLANE)
    sums = exchange(sums.reshape(pieces, 2 * rank // pieces, rank), PLANE).sum(axis=0)
    sums = spread(sums, "z").sum(axis=0)
    sums = spread(sums, PLANE).reshape(2 * rank, rank)

    def whiten(*refs):
        whiten_kernel(node_count, *refs)

    basis, core_matrix = call(
        whiten,
        (jax.ShapeDtypeStruct((width, rank), F32), jax.ShapeDtypeStruct((rank, rank), F32)),
        (VMEM,) * 2,
        (VMEM,) * 2,
        [],
        "whiten",
    )(sums, image)
    return basis[None], core_matrix


def solution(mesh):
    fine = Mesh(mesh.devices.reshape(SIZES), AXES)
    return jax.shard_map(
        body,
        mesh=fine,
        in_specs=(
            P(ROW, COL, None, None, None),
            P(ROW, COL, None),
            P(ROW, COL),
            P(),
            P(AXES, None, None),
            P(AXES, None),
        ),
        out_specs=(P(AXES, None, None), P()),
        check_vma=False,
    )
```

```python
import functools

import jax
import jax.numpy as jnp
from jax import lax
from jax.experimental import pallas as pl
from jax.experimental.pallas import tpu as pltpu
from jax.sharding import Mesh, PartitionSpec as P

EPSILON = 1e-05
AXES = ("yh", "z", "core", "yl", "x")
SIZES = (2, 16, 2, 2, 4)
ROW = ("yh", "z", "core")
COL = ("yl", "x")
PLANE = ("yh", "core", "yl", "x")
GROUP = 19
NO_COST = pl.CostEstimate(flops=0, bytes_accessed=0, transcendentals=0)
VMEM_BYTES = 16 * 1024 * 1024
TILE_VMEM_BYTES = 50 * 1024 * 1024
F32 = jnp.float32
BF16 = jnp.bfloat16


def exchange(array, axis):
    return lax.all_to_all(array, axis, 0, 0, tiled=True)


def spread(array, axis):
    return exchange(jnp.broadcast_to(array[None], (lax.axis_size(axis),) + array.shape), axis)


def swap(array, axis):
    return lax.ppermute(array, axis, [(0, 1), (1, 0)])


def shift(array, axis, step):
    count = lax.axis_size(axis)
    return lax.ppermute(array, axis, [(i, (i + step) % count) for i in range(count)])


def after(array, *others):
    return lax.optimization_barrier((array, *others))[0]


def full_dot(a, b, contract):
    return lax.dot_general(
        a, b, (contract, ((), ())), precision=lax.Precision.HIGHEST, preferred_element_type=F32
    )


def tile_copy(tiles_hbm, tiles, sems, q):
    return pltpu.make_async_copy(tiles_hbm.at[q, 0], tiles.at[q], sems.at[q])


def place_kernel(order_ref, cols_ref, count_ref, place_ref, slot_of):
    rows, slots = cols_ref.shape
    pairs = order_ref.shape[0]
    core, half = lax.axis_index("core"), lax.axis_index("yh")

    def one_pair(p, carry):
        slot_of[order_ref[p]] = p
        return carry

    lax.fori_loop(0, pairs, one_pair, 0, unroll=16)

    def one_row(q, carry):
        count = count_ref[q, 0]
        for s in range(slots):
            natural = cols_ref[q, s]
            upper = natural >= pairs
            slot = slot_of[jnp.where(upper, 2 * pairs - 1 - natural, natural)]
            owner = lax.shift_right_logical(2 * slot + upper.astype(jnp.int32), 3)
            side = 2 * ((owner & 1) ^ core) + ((lax.shift_right_logical(owner, 5) & 1) ^ half)
            place = side * 16 + (lax.shift_right_logical(owner, 1) & 15)
            place_ref[q * slots + s] = jnp.where(s < count, place, 64)
        return carry

    lax.fori_loop(0, rows, one_row, 0)


def scale_kernel(sketch_ref, scale_ref, own_ref, gather_ref):
    sketch = sketch_ref[...].astype(F32)
    scaled = jnp.broadcast_to(scale_ref[...], sketch.shape).T * sketch
    turned, scaled = scaled.T.astype(BF16), scaled.astype(BF16)
    for i in range(own_ref.shape[0]):
        own_ref[i] = turned
    for i in range(gather_ref.shape[0]):
        gather_ref[i] = scaled


def transposed_kernel(pos_ref, count_ref, own_hbm, tiles_hbm, *rest):
    outs, (own_ref, tiles, total, own_sem, tile_sems, out_sems) = rest[:4], rest[4:]
    rows, slots = tiles.shape[0], tiles.shape[1]
    z_count = outs[0].shape[0]
    own_copy = pltpu.make_async_copy(own_hbm, own_ref, own_sem)
    own_copy.start()
    for q in range(rows):
        tile_copy(tiles_hbm, tiles, tile_sems, q).start()
    total[...] = jnp.zeros_like(total)
    own_copy.wait()

    def one_row(q, carry):
        tile_copy(tiles_hbm, tiles, tile_sems, q).wait()
        own = own_ref[q]
        count = count_ref[q, 0]
        for first in range(0, slots, GROUP):
            group = range(first, min(first + GROUP, slots))

            @pl.when(count > first)
            def _(group=group):
                places = [pos_ref[q * slots + s] for s in group]
                terms = [jnp.dot(own, tiles[q, s], preferred_element_type=F32) for s in group]
                before = [total[p] for p in places]
                for p, old, term in zip(places, before, terms):
                    total[p] = old + term

        return carry

    lax.fori_loop(0, rows, one_row, 0)
    copies = [
        pltpu.make_async_copy(total.at[pl.ds(i * z_count, z_count)], out, out_sems.at[i])
        for i, out in enumerate(outs)
    ]
    for copy in copies:
        copy.start()
    for copy in copies:
        copy.wait()


def forward_kernel(pos_ref, count_ref, *rest):
    parts, (tiles_hbm, *outs, tiles, blocks, total, tile_sems, part_sems) = rest[:4], rest[4:]
    rows, slots = tiles.shape[0], tiles.shape[1]
    part = parts[0].shape[0]
    copies = [
        pltpu.make_async_copy(ref, blocks.at[pl.ds(i * part, part)], part_sems.at[i])
        for i, ref in enumerate(parts)
    ]
    for copy in copies:
        copy.start()
    across = len(outs)
    own_half, here = lax.axis_index("yl"), lax.axis_index("x")
    for step in range(across):
        for i in range(2):
            q = (own_half ^ i) * across + ((here + step) & (across - 1))
            tile_copy(tiles_hbm, tiles, tile_sems, q).start()
    blocks[4 * part] = jnp.zeros(blocks.shape[1:], blocks.dtype)
    for copy in copies:
        copy.wait()

    def one_row(i, carry, step, out_ref):
        q = (own_half ^ i) * across + ((here + step) & (across - 1))
        tile_copy(tiles_hbm, tiles, tile_sems, q).wait()
        total[...] = jnp.zeros_like(total)
        for first in range(0, slots, GROUP):
            group = range(first, min(first + GROUP, slots))

            @pl.when(count_ref[q, 0] > first)
            def _(group=group):
                left = jnp.concatenate([tiles[q, s] for s in group], axis=1)
                right = jnp.concatenate([blocks[pos_ref[q * slots + s]] for s in group], axis=0)
                total[...] += jnp.dot(left, right, preferred_element_type=F32)

        out_ref[i] = total[...].astype(out_ref.dtype)
        return carry

    for step, out_ref in enumerate(outs):
        lax.fori_loop(0, 2, functools.partial(one_row, step=step, out_ref=out_ref), 0)


def fore_kernel(keep_ref, *refs):
    got, outs = refs[:-2], refs[-2:]
    for i, out_ref in enumerate(outs):
        total = keep_ref[i]
        for ref in got:
            total = total + ref[i].astype(F32)
        out_ref[...] = total


def image_kernel(back_ref, fore_ref, got_ref, sketch_ref, scale_ref, image_ref, sums_ref):
    back = back_ref[...]
    fore = fore_ref[...] + got_ref[...]
    sketch = sketch_ref[...].astype(F32)
    scale = jnp.broadcast_to(scale_ref[...], sketch.shape).T
    image = sketch - scale * (fore + back.T)
    image_ref[...] = image
    width = image.shape[1]
    sums_ref[0:width, :] = full_dot(image, image, ((0,), (0,)))
    sums_ref[width:, :] = full_dot(sketch, image, ((0,), (0,)))


def whiten_kernel(node_count, sums_ref, image_ref, basis_ref, core_ref):
    width = image_ref.shape[1]
    line = lax.broadcasted_iota(jnp.int32, (width, width), 0)
    lane = lax.broadcasted_iota(jnp.int32, (width, width), 1)
    eye = jnp.where(line == lane, 1.0, 0.0).astype(F32)
    gram = sums_ref[0:width, :] / node_count + EPSILON * eye
    cross = sums_ref[width:, :] / node_count
    cross = 0.5 * (cross + cross.T)
    step = 8
    bands = width // step
    left = [gram[step * k : step * (k + 1), :] for k in range(bands)]
    right = [eye[step * k : step * (k + 1), :] for k in range(bands)]
    sub = lax.broadcasted_iota(jnp.int32, (step, width), 0)

    def line_of(band, i):
        return jnp.broadcast_to(band[i : i + 1, :], (step, width))

    def lane_of(band, j):
        return jnp.broadcast_to(band[:, j : j + 1], (step, width))

    whitener = []
    for at in range(bands):
        first = step * at
        lanes = [lane_of(left[at], first + i) for i in range(step)]
        block = [[line_of(lanes[j], i) for j in range(i + 1)] for i in range(step)]
        lower = [[None] * step for _ in range(step)]
        inverse = []
        for j in range(step):
            inverse.append(1.0 / block[j][j])
            for i in range(j + 1, step):
                lower[i][j] = block[i][j] * inverse[j]
            for i in range(j + 1, step):
                for k in range(j + 1, i + 1):
                    block[i][k] = block[i][k] - lower[i][j] * block[k][j]
        solved = []
        for band in (left[at], right[at]):
            lines = [line_of(band, i) for i in range(step)]
            for j in range(step):
                for i in range(j + 1, step):
                    lines[i] = lines[i] - lower[i][j] * lines[j]
            solved.append(lines)
        scaled = jnp.zeros((step, width), F32)
        for i in range(step):
            scaled = jnp.where(sub == i, solved[1][i] * lax.rsqrt(block[i][i]), scaled)
        whitener.append(scaled)
        if at + 1 == bands:
            break
        for lines in solved:
            for i in range(step):
                lines[i] = lines[i] * inverse[i]
            for j in reversed(range(step)):
                for i in range(j):
                    lines[i] = lines[i] - lower[j][i] * lines[j]
        for k in range(at + 1, bands):
            lanes = [lane_of(left[k], first + i) for i in range(step)]
            for i in range(step):
                left[k] = left[k] - lanes[i] * solved[0][i]
                right[k] = right[k] - lanes[i] * solved[1][i]
    whitener = jnp.concatenate(whitener, axis=0)
    basis_ref[...] = full_dot(image_ref[...], whitener, ((1,), (1,)))
    half_way = full_dot(whitener, cross, ((1,), (0,)))
    core_ref[...] = full_dot(half_way, whitener, ((1,), (1,)))


def spec(space):
    return pl.BlockSpec(memory_space=space)


def call(kernel, out_shape, in_spaces, out_spaces, scratch, name, cost=NO_COST, vmem=VMEM_BYTES):
    many = isinstance(out_spaces, tuple)
    return pl.pallas_call(
        kernel,
        out_shape=out_shape,
        in_specs=[spec(s) for s in in_spaces],
        out_specs=tuple(spec(s) for s in out_spaces) if many else spec(out_spaces),
        scratch_shapes=scratch,
        compiler_params=pltpu.CompilerParams(vmem_limit_bytes=vmem),
        cost_estimate=cost,
        name=name,
    )


def body(graph_tiles, tile_cols, tile_counts, pair_order, sketch, degree_scale):
    rows, _, slots, width, _ = graph_tiles.shape
    rank = sketch.shape[2]
    pairs = pair_order.shape[0]
    node_count = 2 * pairs * width
    z_count = lax.axis_size("z")
    HBM, VMEM, SMEM = pltpu.HBM, pltpu.VMEM, pltpu.SMEM

    own_rows, gather = call(
        scale_kernel,
        (
            jax.ShapeDtypeStruct((lax.axis_size(COL), rank, width), BF16),
            jax.ShapeDtypeStruct((z_count, width, rank), BF16),
        ),
        (VMEM,) * 2,
        (VMEM,) * 2,
        [],
        "scale",
    )(sketch[0], degree_scale)
    tile_scratch = pltpu.VMEM((rows, slots, width, width), BF16)
    row_sems = pltpu.SemaphoreType.DMA((rows,))
    part_sems = pltpu.SemaphoreType.DMA((4,))
    part = jax.ShapeDtypeStruct((z_count, rank, width), F32)

    places = call(
        place_kernel,
        jax.ShapeDtypeStruct((rows * slots,), jnp.int32),
        (SMEM, SMEM, SMEM),
        SMEM,
        [pltpu.SMEM((pairs,), jnp.int32)],
        "places",
    )(pair_order, tile_cols[:, 0, :], tile_counts)
    own_rows = exchange(own_rows, COL)
    gather = exchange(after(gather, places), "z")
    near, far, near_send, far_send = call(
        transposed_kernel,
        (part,) * 4,
        (SMEM, SMEM, HBM, HBM),
        (HBM,) * 4,
        [
            pltpu.VMEM((rows, rank, width), BF16),
            tile_scratch,
            pltpu.VMEM((4 * z_count + 1, rank, width), F32),
            pltpu.SemaphoreType.DMA,
            row_sems,
            part_sems,
        ],
        "transposed_products",
        vmem=TILE_VMEM_BYTES,
    )(places, tile_counts, own_rows, graph_tiles)
    far_got = swap(far_send, "core")
    near_got = swap(near_send, "core")
    far = (far + far_got).astype(BF16)
    near = lax.optimization_barrier(near + near_got)
    back = (near + swap(far, "yh").astype(F32)).astype(BF16)
    gather = after(gather, far, near_got)
    gather1 = after(swap(gather, "yh"), back)
    gather2 = swap(gather, "core")
    gather3 = swap(gather1, "core")
    back = exchange(after(back, gather2), "z")
    pair = (2, width, rank)
    fore, *sends = call(
        forward_kernel,
        (jax.ShapeDtypeStruct(pair, F32),) + (jax.ShapeDtypeStruct(pair, BF16),) * 3,
        (SMEM, SMEM) + (HBM,) * 5,
        (VMEM,) * 4,
        [
            tile_scratch,
            pltpu.VMEM((4 * z_count + 1, width, rank), BF16),
            pltpu.VMEM((width, rank), F32),
            row_sems,
            part_sems,
        ],
        "forward_products",
        pl.CostEstimate(flops=12650000000, bytes_accessed=0, transcendentals=0),
        TILE_VMEM_BYTES,
    )(places, tile_counts, gather, gather1, gather2, gather3, graph_tiles)
    got = [shift(send, "x", step) for step, send in enumerate(sends, 1)]
    whole = jax.ShapeDtypeStruct((width, rank), F32)
    fore, other = call(fore_kernel, (whole,) * 2, (VMEM,) * 4, (VMEM,) * 2, [], "fore_sum")(fore, *got)
    got = swap(other, "yl")
    back = back.astype(F32).sum(axis=0)

    image, sums = call(
        image_kernel,
        (jax.ShapeDtypeStruct((width, rank), F32), jax.ShapeDtypeStruct((2 * rank, rank), F32)),
        (VMEM,) * 5,
        (VMEM,) * 2,
        [],
        "image_and_grams",
    )(back, fore, got, sketch[0], degree_scale)

    pieces = lax.axis_size(PLANE)
    sums = exchange(sums.reshape(pieces, 2 * rank // pieces, rank), PLANE).sum(axis=0)
    sums = spread(sums, "z").sum(axis=0)
    sums = spread(sums, PLANE).reshape(2 * rank, rank)

    def whiten(*refs):
        whiten_kernel(node_count, *refs)

    basis, core_matrix = call(
        whiten,
        (jax.ShapeDtypeStruct((width, rank), F32), jax.ShapeDtypeStruct((rank, rank), F32)),
        (VMEM,) * 2,
        (VMEM,) * 2,
        [],
        "whiten",
    )(sums, image)
    return basis[None], core_matrix


def solution(mesh):
    fine = Mesh(mesh.devices.reshape(SIZES), AXES)
    return jax.shard_map(
        body,
        mesh=fine,
        in_specs=(
            P(ROW, COL, None, None, None),
            P(ROW, COL, None),
            P(ROW, COL),
            P(),
            P(AXES, None, None),
            P(AXES, None),
        ),
        out_specs=(P(AXES, None, None), P()),
        check_vma=False,
    )
```
